32 devices in a mesh: seq: 8 (over y, x, core), head: 4 (over z).
Axes of the slice: x: 2, y: 2, z: 4, core: 2. Of those that a mesh axis runs over, the one named last changes fastest.
Arguments:
- cached_keys: bfloat16 [32768, 4096], P(('seq', 'head')), may hold values from -48 to 48
- sketch_matrix: bfloat16 [4096, 512], replicated, may hold values from -0.09375 to 0.09375
- cached_values: bfloat16 [32768, 4096], P('seq', 'head'), may hold values from -6 to 6
- queries: bfloat16 [8, 128, 128], P('head'), may hold values from -64 to 64
- new_keys: bfloat16 [4, 4096], P(None, 'head'), may hold values from -8.25 to 8.25
- new_values: bfloat16 [4, 4096], P(None, 'head'), may hold values from -6 to 6
Outputs:
- attended: bfloat16 [8, 128, 128], P('head', 'seq')
- key_bases: bfloat16 [32768, 512], P(('seq', 'head'))
- coefficients: bfloat16 [4096, 512], P('head')
The draws below stay inside these ranges and needn't reach their ends.
All inputs are finite; a program needn't handle non-finite values.
Results may differ from the reference program's by a relative error of at most 0.01145.
The reference program's roundings to bfloat16 on the way (of `stored_ortho`, `absorbed` and `weights_bf`) count: a program that leaves them out, or rounds other values in their place, can miss the bound.
Values may be sent and summed in bfloat16 or wider, within the bound.
A program may use at most 128 MiB of HBM per device.

```python
import math
import jax
import jax.numpy as jnp
from jax import lax

KVH = 8
HD = 128
GQA = 8
RANK = 512
LAYERS = 4
STEPS = 4
TOKENS = 32768
C = 4096
QPER = 128


def draw_new_keys(key, part):
    key = jax.random.fold_in(key, 3)
    gaussian = jnp.clip(jax.random.normal(key, (STEPS, C), jnp.float32), -4.0, 4.0)
    stacked = gaussian
    return (2.0 * stacked).astype(jnp.bfloat16)


def draw_queries(key, part):
    key = jax.random.fold_in(key, 5)
    gaussian = jnp.clip(jax.random.normal(key, (KVH, LAYERS, STEPS, GQA, HD), jnp.float32), -4.0, 4.0) * 6.0
    return gaussian.reshape(KVH, QPER, HD).astype(jnp.bfloat16)


def draw_cached_keys(key, part):
    key = jax.random.fold_in(key, 7)
    noise_key, row_key, col_key = jax.random.split(key, 3)
    gaussian = jnp.clip(jax.random.normal(noise_key, (TOKENS, C), jnp.float32), -4.0, 4.0)
    row_scale = 0.5 * jnp.exp(jax.random.uniform(row_key, (TOKENS, 1), jnp.float32, 0.0, math.log(4.0)))
    col_scale = 0.5 * jnp.exp(jax.random.uniform(col_key, (1, C), jnp.float32, 0.0, math.log(4.0)))
    drawn = row_scale * gaussian * col_scale
    return drawn.astype(jnp.bfloat16)


def levels(rng, shape, pieces, smallest, high):
    factor_of, own = 1.0, jax.random.fold_in(rng, 6)
    for position, blocks in pieces:
        heights = jnp.exp(jax.random.uniform(jax.random.fold_in(own, position), (blocks,), jnp.float32, smallest / len(pieces), high / len(pieces)))
        factor_of = factor_of * jnp.repeat(heights, shape[position] // blocks).reshape([-1 if axis == position else 1 for axis in range(len(shape))])
    return factor_of


def scatter_about(rng, dims, spread, limit, shards=(), kind=jnp.bfloat16):
    result = jax.random.normal(rng, dims, jnp.float32) * spread
    if len(shards) > 0:
        result = levels(rng, dims, shards, -0.22, 0.18) * result
    return jnp.clip(result, min=-limit, max=limit).astype(kind)


def setup_inputs(seed: int = 0) -> dict:
    seeds = jax.random.split(jax.random.key(seed), 7)
    cached_keys = draw_cached_keys(jax.random.fold_in(seeds[6], 71), 0)
    sketch_matrix = scatter_about(seeds[1], (C, RANK), C ** -0.5, 0.09375)
    cached_values = scatter_about(seeds[2], (TOKENS, C), 1.0, 6.0, ((0, 8), (1, 4)))
    queries = draw_queries(jax.random.fold_in(seeds[6], 71), 0)
    new_keys = draw_new_keys(jax.random.fold_in(seeds[6], 71), 0)
    new_values = scatter_about(seeds[5], (STEPS, C), 1.0, 6.0, ((1, 4),))
    return {"cached_keys": cached_keys, "sketch_matrix": sketch_matrix, "cached_values": cached_values, "queries": queries, "new_keys": new_keys, "new_values": new_values}


def right_solve(lower_factor, matrix):
    return lax.linalg.triangular_solve(lower_factor, matrix, left_side=False, lower=True, transpose_a=True)

def reference(cached_keys, sketch_matrix, cached_values, queries, new_keys, new_values):
    highest = lax.Precision.HIGHEST
    sketch = jnp.dot(cached_keys.astype(jnp.float32), sketch_matrix.astype(jnp.float32), preferred_element_type=jnp.float32)
    gram_first = jnp.dot(sketch.T, sketch, precision=highest)
    lower_first = jnp.linalg.cholesky(gram_first)
    orthonormal = right_solve(lower_first, sketch)
    stored_ortho = orthonormal.astype(jnp.bfloat16)
    coef_full = lax.dot_general(cached_keys.astype(jnp.float32), stored_ortho.astype(jnp.float32), (((0,), (0,)), ((), ())), preferred_element_type=jnp.float32)
    gram_second = jnp.dot(coef_full.T, coef_full, precision=highest)
    lower_second = jnp.linalg.cholesky(gram_second)
    coefficients = right_solve(lower_second, coef_full).astype(jnp.bfloat16)
    key_bases = jnp.dot(orthonormal, lower_second, precision=highest).astype(jnp.bfloat16)
    score_scale = 1.0 / math.sqrt(HD)
    head_width = LAYERS * HD
    rows_layer = STEPS * GQA
    step_of_row = jnp.arange(rows_layer) // GQA
    allowed = step_of_row[:, None] >= jnp.arange(STEPS)[None, :]

    def one_head(head_index):
        column_start = (head_index * head_width).astype(jnp.int32)
        query_rows = lax.dynamic_index_in_dim(queries, head_index, 0, keepdims=False).reshape(LAYERS, rows_layer, HD)
        head_coef = lax.dynamic_slice_in_dim(coefficients, column_start, head_width, 0).reshape(LAYERS, HD, RANK)
        absorbed = (jnp.einsum('lqh,lhr->lqr', query_rows.astype(jnp.float32), head_coef.astype(jnp.float32)) * score_scale).astype(jnp.bfloat16)
        cache_scores = jnp.dot(absorbed.reshape(LAYERS * rows_layer, RANK).astype(jnp.float32), key_bases.T.astype(jnp.float32), preferred_element_type=jnp.float32)
        head_keys = lax.dynamic_slice_in_dim(new_keys, column_start, head_width, 1).reshape(STEPS, LAYERS, HD)
        new_scores = jnp.einsum('lqh,ulh->lqu', query_rows.astype(jnp.float32), head_keys.astype(jnp.float32)) * score_scale
        new_scores = jnp.where(allowed[None], new_scores, -jnp.inf).reshape(LAYERS * rows_layer, STEPS)
        highest_score = jnp.maximum(lax.optimization_barrier(jnp.max(cache_scores, axis=1)), lax.optimization_barrier(jnp.max(new_scores, axis=1)))
        cache_weights = jnp.exp(cache_scores - highest_score[:, None])
        new_weights = jnp.exp(new_scores - highest_score[:, None])
        softmax_total = lax.optimization_barrier(jnp.sum(cache_weights, axis=1)) + lax.optimization_barrier(jnp.sum(new_weights, axis=1))
        weights_bf = cache_weights.astype(jnp.bfloat16).reshape(LAYERS, rows_layer, -1)
        head_values = lax.dynamic_slice_in_dim(cached_values, column_start, head_width, 1)
        numerator = jnp.stack([jnp.dot(weights_bf[layer_index].astype(jnp.float32), head_values[:, layer_index * HD:(layer_index + 1) * HD].astype(jnp.float32), preferred_element_type=jnp.float32) for layer_index in range(LAYERS)])
        fresh_values = lax.dynamic_slice_in_dim(new_values, column_start, head_width, 1).astype(jnp.float32).reshape(STEPS, LAYERS, HD)
        fresh_part = lax.optimization_barrier(jnp.sum(new_weights.reshape(LAYERS, rows_layer, STEPS)[..., None] * jnp.transpose(fresh_values, (1, 0, 2))[:, None], axis=2))
        result_rows = (numerator + fresh_part) / softmax_total.reshape(LAYERS, rows_layer)[..., None]
        return result_rows.astype(jnp.bfloat16).reshape(QPER, HD)
    attended = lax.map(one_head, jnp.arange(KVH, dtype=jnp.int32))
    return (attended, key_bases, coefficients)
```

```python
import functools
import math

import jax
import jax.numpy as jnp
from jax import lax
from jax.experimental import pallas as pl
from jax.experimental.pallas import tpu as pltpu
from jax.sharding import PartitionSpec as P

GQA = 8
LAYERS = 4
STEPS = 4
HI = lax.Precision.HIGHEST
BLK = 128

def eliminate(square):
    groups = BLK // 8
    sub = lax.broadcasted_iota(jnp.int32, (8, BLK), 0)
    lane = lax.broadcasted_iota(jnp.int32, (8, BLK), 1)
    s = [square[8 * g:8 * g + 8, :] for g in range(groups)]
    w = [(lane == sub + 8 * g).astype(jnp.float32) for g in range(groups)]
    for j in range(BLK):
        gj, r = divmod(j, 8)
        row = s[gj][r:r + 1, :]
        inv = 1.0 / jnp.broadcast_to(row[:, j:j + 1], (1, BLK))
        srow = jnp.broadcast_to(row * inv, (8, BLK))
        wrow = jnp.broadcast_to(w[gj][r:r + 1, :] * inv, (8, BLK))
        for g in range(gj, groups):
            if g == gj and r == 7:
                continue
            col = jnp.broadcast_to(s[g][:, j:j + 1], (8, BLK))
            if g == gj:
                col = jnp.where(sub > r, col, 0.0)
            s[g] = s[g] - col * srow
            w[g] = w[g] - col * wrow
    out = []
    for g in range(groups):
        diag = jnp.sum(jnp.where(lane == sub + 8 * g, s[g], 0.0), axis=1, keepdims=True)
        out.append(w[g] * lax.rsqrt(diag))
    return jnp.concatenate(out, axis=0)

def factor(mat, size):
    n = size // BLK
    lane = lax.broadcasted_iota(jnp.int32, (BLK, 2 * size), 1)

    def panel(k, carry):
        r0 = pl.multiple_of(k * BLK, BLK)
        inv = eliminate(mat[pl.ds(r0, BLK), pl.ds(r0, BLK)])
        solved = jnp.dot(inv, mat[pl.ds(r0, BLK), :], precision=HI, preferred_element_type=jnp.float32)
        mat[pl.ds(r0, BLK), :] = jnp.where(lane >= r0, solved, 0.0)

        def below(i, c):
            i0 = pl.multiple_of(i * BLK, BLK)
            mat[pl.ds(i0, BLK), :] -= lax.dot_general(
                mat[pl.ds(r0, BLK), pl.ds(i0, BLK)], mat[pl.ds(r0, BLK), :],
                (((0,), (0,)), ((), ())), precision=HI, preferred_element_type=jnp.float32)
            return c
        lax.fori_loop(k + 1, n, below, 0)
        return carry
    lax.fori_loop(0, n, panel, 0)

def kernel(size, g_ref, u_ref, v_ref, mat):
    r = lax.broadcasted_iota(jnp.int32, (size, size), 0)
    c = lax.broadcasted_iota(jnp.int32, (size, size), 1)
    mat[:, :size] = g_ref[...]
    mat[:, size:] = (r == c).astype(jnp.float32)
    factor(mat, size)
    u_ref[...] = jnp.where(c >= r, mat[:, :size], 0.0)
    v_ref[...] = mat[:, size:]

def chol_inv(g):
    size = g.shape[0]
    return pl.pallas_call(
        functools.partial(kernel, size),
        out_shape=[jax.ShapeDtypeStruct((size, size), jnp.float32)] * 2,
        in_specs=[pl.BlockSpec(memory_space=pltpu.VMEM)],
        out_specs=[pl.BlockSpec(memory_space=pltpu.VMEM)] * 2,
        scratch_shapes=[pltpu.VMEM((size, 2 * size), jnp.float32)],
        compiler_params=pltpu.CompilerParams(vmem_limit_bytes=32 << 20),
    )(g)


def joined(part, axis, combine):
    gathered = jax.tree.map(lambda a: lax.all_gather(a, axis), part)

    def take(source):
        return jax.tree.map(lambda a: lax.dynamic_index_in_dim(a, source, 0, False), gathered)

    return lax.fori_loop(
        1, lax.axis_size(axis), lambda source, state: combine(state, take(source)), take(0)
    )


def soft_join(former, latter):
    joint_peak = jnp.maximum(former[0], latter[0])
    former_factor = jnp.exp(former[0] - joint_peak)
    latter_factor = jnp.exp(latter[0] - joint_peak)
    return (
        joint_peak,
        former[1] * former_factor + latter[1] * latter_factor,
        former[2] * former_factor[..., None] + latter[2] * latter_factor[..., None],
    )


def per_device(cached_keys, sketch_matrix, cached_values, queries, new_keys, new_values):
    highest = lax.Precision.HIGHEST
    seq_count = lax.axis_size("seq")
    head_count = lax.axis_size("head")
    tok_rows, key_width = cached_keys.shape
    sketch_rank = sketch_matrix.shape[1]
    contract = (((0,), (0,)), ((), ()))
    sketch = jnp.dot(cached_keys, sketch_matrix, preferred_element_type=jnp.float32)
    gram_first = lax.psum(jnp.dot(sketch.T, sketch, precision=highest), ("seq", "head"))
    _, inverse_first = chol_inv(gram_first)
    rows_with_rows = (((1,), (1,)), ((), ()))
    orthonormal = lax.dot_general(sketch, inverse_first, rows_with_rows, precision=highest)
    stored_ortho = orthonormal.astype(jnp.bfloat16)
    coef_rows = lax.psum_scatter(
        lax.dot_general(cached_keys, stored_ortho, contract, preferred_element_type=jnp.float32),
        ("head", "seq"),
        scatter_dimension=0,
        tiled=True,
    )
    gram_second = lax.psum(jnp.dot(coef_rows.T, coef_rows, precision=highest), ("seq", "head"))
    upper_second, inverse_second = chol_inv(gram_second)
    coef_piece = lax.dot_general(
        coef_rows, inverse_second, rows_with_rows, precision=highest
    ).astype(jnp.bfloat16)
    coefficients = lax.all_gather(coef_piece, "seq", axis=0, tiled=True)
    key_bases = lax.dot_general(
        orthonormal, upper_second, rows_with_rows, precision=highest
    ).astype(jnp.bfloat16)
    heads_here, query_rows, head_dim = queries.shape
    rows_layer = STEPS * GQA
    score_scale = 1.0 / math.sqrt(head_dim)
    query_view = queries.reshape(heads_here, LAYERS, rows_layer, head_dim)
    coef_view = coefficients.reshape(heads_here, LAYERS, head_dim, sketch_rank)
    absorbed = (
        jnp.einsum("klqh,klhr->klqr", query_view, coef_view, preferred_element_type=jnp.float32)
        * score_scale
    ).astype(jnp.bfloat16)
    flat_queries = absorbed.reshape(heads_here * query_rows, sketch_rank)
    cache_scores = lax.dot_general(
        flat_queries,
        lax.all_gather(key_bases, "head", axis=0, tiled=True),
        (((1,), (1,)), ((), ())),
        preferred_element_type=jnp.float32,
    )
    local_peak = jnp.max(cache_scores, axis=1)
    cache_weights = jnp.exp(cache_scores - local_peak[:, None])
    local_total = jnp.sum(cache_weights, axis=1)
    weights_bf = cache_weights.astype(jnp.bfloat16).reshape(heads_here, LAYERS, rows_layer, -1)
    value_view = cached_values.reshape(cached_values.shape[0], heads_here, LAYERS, head_dim)
    numerator = jnp.einsum(
        "klqn,nklh->klqh", weights_bf, value_view, preferred_element_type=jnp.float32
    ).reshape(heads_here, query_rows, head_dim)
    row_peaks = local_peak.reshape(heads_here, query_rows)
    totals = local_total.reshape(heads_here, query_rows)
    own_rows = query_rows // seq_count
    row_begin = lax.axis_index("seq") * own_rows
    row_peaks, totals, numerator = joined((row_peaks, totals, numerator), "seq", soft_join)
    row_peaks = lax.dynamic_slice_in_dim(row_peaks, row_begin, own_rows, 1)
    totals = lax.dynamic_slice_in_dim(totals, row_begin, own_rows, 1)
    numerator = lax.dynamic_slice_in_dim(numerator, row_begin, own_rows, 1)
    row_index = row_begin + jnp.arange(own_rows, dtype=jnp.int32)
    layer_of_row = row_index // rows_layer
    step_of_row = row_index // GQA % STEPS
    layer_pick = (layer_of_row[:, None] == jnp.arange(LAYERS, dtype=jnp.int32)[None, :]).astype(
        jnp.float32
    )
    allowed = step_of_row[:, None] >= jnp.arange(STEPS, dtype=jnp.int32)[None, :]
    own_queries = lax.dynamic_slice_in_dim(queries, row_begin, own_rows, 1)
    fresh_keys = new_keys.reshape(STEPS, heads_here, LAYERS, head_dim)
    fresh_all = (
        jnp.einsum("kqh,uklh->kqul", own_queries, fresh_keys, preferred_element_type=jnp.float32)
        * score_scale
    )
    fresh_scores = jnp.sum(fresh_all * layer_pick[None, :, None, :], axis=3)
    fresh_scores = jnp.where(allowed[None], fresh_scores, -jnp.inf)
    overall = jnp.maximum(row_peaks, jnp.max(fresh_scores, axis=2))
    cache_factor = jnp.exp(row_peaks - overall)
    fresh_weights = jnp.exp(fresh_scores - overall[..., None])
    fresh_vals = jnp.transpose(
        new_values.astype(jnp.float32).reshape(STEPS, heads_here, LAYERS, head_dim), (1, 0, 2, 3)
    )
    picked = jnp.sum(layer_pick[None, :, None, :, None] * fresh_vals[:, None], axis=3)
    fresh_part = jnp.sum(fresh_weights[..., None] * picked, axis=2)
    softmax_total = totals * cache_factor + jnp.sum(fresh_weights, axis=2)
    attended = (
        (numerator * cache_factor[..., None] + fresh_part) / softmax_total[..., None]
    ).astype(jnp.bfloat16)
    return (attended, key_bases, coefficients)


def solution(mesh):
    placed = (
        P(("seq", "head"), None),
        P(),
        P("seq", "head"),
        P("head", None, None),
        P(None, "head"),
        P(None, "head"),
    )
    return jax.shard_map(
        per_device,
        mesh=mesh,
        in_specs=placed,
        out_specs=(P("head", "seq", None), P(("seq", "head"), None), P("head", None)),
        check_vma=False,
    )
```

```python
import functools
import math

import jax
import jax.numpy as jnp
from jax import lax
from jax.experimental import pallas as pl
from jax.experimental.pallas import tpu as pltpu
from jax.sharding import PartitionSpec as P

GQA = 8
LAYERS = 4
STEPS = 4
HI = lax.Precision.HIGHEST
BLK = 128

def eliminate(square):
    groups = BLK // 8
    sub = lax.broadcasted_iota(jnp.int32, (8, BLK), 0)
    lane = lax.broadcasted_iota(jnp.int32, (8, BLK), 1)
    s = [square[8 * g:8 * g + 8, :] for g in range(groups)]
    w = [(lane == sub + 8 * g).astype(jnp.float32) for g in range(groups)]
    for j in range(BLK):
        gj, r = divmod(j, 8)
        row = s[gj][r:r + 1, :]
        inv = 1.0 / jnp.broadcast_to(row[:, j:j + 1], (1, BLK))
        srow = jnp.broadcast_to(row * inv, (8, BLK))
        wrow = jnp.broadcast_to(w[gj][r:r + 1, :] * inv, (8, BLK))
        for g in range(gj, groups):
            if g == gj and r == 7:
                continue
            col = jnp.broadcast_to(s[g][:, j:j + 1], (8, BLK))
            if g == gj:
                col = jnp.where(sub > r, col, 0.0)
            s[g] = s[g] - col * srow
            w[g] = w[g] - col * wrow
    out = []
    for g in range(groups):
        diag = jnp.sum(jnp.where(lane == sub + 8 * g, s[g], 0.0), axis=1, keepdims=True)
        out.append(w[g] * lax.rsqrt(diag))
    return jnp.concatenate(out, axis=0)

def factor(mat, size):
    n = size // BLK
    lane = lax.broadcasted_iota(jnp.int32, (BLK, 2 * size), 1)

    def panel(k, carry):
        r0 = pl.multiple_of(k * BLK, BLK)
        inv = eliminate(mat[pl.ds(r0, BLK), pl.ds(r0, BLK)])
        solved = jnp.dot(inv, mat[pl.ds(r0, BLK), :], precision=HI, preferred_element_type=jnp.float32)
        mat[pl.ds(r0, BLK), :] = jnp.where(lane >= r0, solved, 0.0)

        def below(i, c):
            i0 = pl.multiple_of(i * BLK, BLK)
            mat[pl.ds(i0, BLK), :] -= lax.dot_general(
                mat[pl.ds(r0, BLK), pl.ds(i0, BLK)], mat[pl.ds(r0, BLK), :],
                (((0,), (0,)), ((), ())), precision=HI, preferred_element_type=jnp.float32)
            return c
        lax.fori_loop(k + 1, n, below, 0)
        return carry
    lax.fori_loop(0, n, panel, 0)

def log2(count):
    return count.bit_length() - 1


class Hypercube:
    def __init__(self, seq_count, head_count):
        self.seq = lax.axis_index("seq")
        self.head = lax.axis_index("head")
        self.seq_bits = [("seq", k) for k in range(log2(seq_count))]
        self.head_bits = [("head", k) for k in range(log2(head_count))]
        rest = self.seq_bits[1:] + self.head_bits
        swapped = self.seq_bits[1:][::-1] + self.head_bits[::-1]
        self.orders = [self.seq_bits[:1] + rest, self.seq_bits[:1] + swapped]

    def bit(self, which):
        axis, k = which
        return (self.seq if axis == "seq" else self.head) // (1 << k) % 2

    def partner(self, which):
        axis, k = which
        step = (1 - 2 * self.bit(which)) * (1 << k)
        if axis == "seq":
            return (self.seq + step, self.head)
        return (self.seq, self.head + step)

    def greet(self):
        barrier = pltpu.get_barrier_semaphore()
        bits = self.seq_bits + self.head_bits
        for which in bits:
            pl.semaphore_signal(
                barrier, inc=1, device_id=self.partner(which), device_id_type=pl.DeviceIdType.MESH
            )
        pl.semaphore_wait(barrier, len(bits))

    def copy(self, source, target, send_sem, recv_sem, which):
        return pltpu.make_async_remote_copy(
            src_ref=source,
            dst_ref=target,
            send_sem=send_sem,
            recv_sem=recv_sem,
            device_id=self.partner(which),
            device_id_type=pl.DeviceIdType.MESH,
        )


def add_rows(target, start, source, offset, rows, columns):
    step = min(rows, 64)

    def add(i, carry):
        t0 = pl.multiple_of(start + i * step, step)
        s0 = pl.multiple_of(offset + i * step, step)
        target[pl.ds(t0, step), columns] += source[pl.ds(s0, step), columns]
        return carry

    lax.fori_loop(0, rows // step, add, 0)


def part_columns(width):
    return [pl.ds(0, width // 2), pl.ds(width // 2, width // 2)]


def halving_plan(rows, count):
    plan, offset = [], 0
    for _ in range(count):
        split = rows >= 16
        rows = rows // 2 if split else rows
        plan.append((split, rows, offset))
        offset += rows
    return plan, offset


def halve(cube, buf, recv, plan, send_sem, recv_sem):
    columns = part_columns(buf.shape[1])
    starts = [0, 0]
    sent = []
    for level, (split, rows, offset) in enumerate(plan):
        copies = []
        for part, order in enumerate(cube.orders):
            which = order[level]
            bit = cube.bit(which)
            go = starts[part] + (1 - bit) * rows if split else starts[part]
            if split:
                starts[part] = starts[part] + bit * rows
            copies.append(
                cube.copy(
                    buf.at[pl.ds(pl.multiple_of(go, 8), rows), columns[part]],
                    recv.at[pl.ds(offset, rows), columns[part]],
                    send_sem.at[level, part],
                    recv_sem.at[level, part],
                    which,
                )
            )
        for copy in copies:
            copy.start()
        for part, copy in enumerate(copies):
            copy.wait_recv()
            if not split:
                copy.wait_send()
            else:
                sent.append(copy)
            add_rows(buf, starts[part], recv, offset, rows, columns[part])
    for copy in sent:
        copy.wait_send()
    return starts


def double(cube, buf, full, plan, starts, send_sem, recv_sem):
    columns = part_columns(buf.shape[1])
    rows = plan[-1][1]
    for part in range(2):
        here = pl.ds(pl.multiple_of(starts[part], 8), rows)
        full[here, columns[part]] = buf[here, columns[part]]
    starts = list(starts)
    sent = []
    for level in reversed(range(len(plan))):
        split, rows, _ = plan[level]
        if not split:
            continue
        copies = []
        for part, order in enumerate(cube.orders):
            which = order[level]
            here = full.at[pl.ds(pl.multiple_of(starts[part], 8), rows), columns[part]]
            copies.append(
                cube.copy(here, here, send_sem.at[level, part], recv_sem.at[level, part], which)
            )
            starts[part] = starts[part] - cube.bit(which) * rows
        for copy in copies:
            copy.start()
        for copy in copies:
            copy.wait_recv()
        sent += copies
    for copy in sent:
        copy.wait_send()


def load_augmented(mat, full, size):
    r = lax.broadcasted_iota(jnp.int32, (size, size), 0)
    c = lax.broadcasted_iota(jnp.int32, (size, size), 1)
    mat[:, :size] = full[...]
    mat[:, size:] = (r == c).astype(jnp.float32)


def upper_part(mat, size):
    r = lax.broadcasted_iota(jnp.int32, (size, size), 0)
    c = lax.broadcasted_iota(jnp.int32, (size, size), 1)
    return jnp.where(c >= r, mat[:, :size], 0.0)


def first_kernel(seq_count, head_count, g_ref, v_ref, buf, recv, full, mat, rs, rr, gs, gr):
    size = g_ref.shape[0]
    cube = Hypercube(seq_count, head_count)
    cube.greet()
    plan, _ = halving_plan(size, len(cube.orders[0]))
    buf[...] = g_ref[...]
    starts = halve(cube, buf, recv, plan, rs, rr)
    double(cube, buf, full, plan, starts, gs, gr)
    load_augmented(mat, full, size)
    factor(mat, size)
    v_ref[...] = mat[:, size:]


def scratch_of(size, count):
    _, total = halving_plan(size, count)
    sems = pltpu.SemaphoreType.DMA((count, 2))
    return [
        pltpu.VMEM((size, size), jnp.float32),
        pltpu.VMEM((total, size), jnp.float32),
        pltpu.VMEM((size, size), jnp.float32),
        pltpu.VMEM((size, 2 * size), jnp.float32),
        sems,
        sems,
        sems,
        sems,
    ]


def summed_inverse(gram, seq_count, head_count):
    size = gram.shape[0]
    return pl.pallas_call(
        functools.partial(first_kernel, seq_count, head_count),
        out_shape=jax.ShapeDtypeStruct((size, size), jnp.float32),
        in_specs=[pl.BlockSpec(memory_space=pltpu.VMEM)],
        out_specs=pl.BlockSpec(memory_space=pltpu.VMEM),
        scratch_shapes=scratch_of(size, log2(seq_count * head_count)),
        compiler_params=pltpu.CompilerParams(
            collective_id=0, has_side_effects=True, vmem_limit_bytes=24 << 20
        ),
        cost_estimate=pl.CostEstimate(
            flops=100_000_000_000, bytes_accessed=4_000_000, transcendentals=0
        ),
    )(gram)


def second_kernel(
    seq_count, head_count, k_ref, o_ref, c_ref, u_ref, v_ref,
    part_sum, part_recv, buf, recv, full, mat, rs, rr, gs, gr, cs, cr, as_, ar,
):
    size = o_ref.shape[1]
    cube = Hypercube(seq_count, head_count)
    cube.greet()
    columns = part_columns(size)
    width = k_ref.shape[1]
    own = width // (seq_count * head_count)
    count = len(cube.orders[0])
    chunk = max(own, 128)
    pieces = chunk // own

    def place(block, order):
        at = 0
        for level, (axis, k) in enumerate(order):
            bit = block // ((1 << k) * (1 if axis == "seq" else seq_count)) % 2
            at = at + bit * (1 << (count - 1 - level))
        return pl.multiple_of(at * own, own)

    def product(index, carry):
        c0 = pl.multiple_of(index * chunk, chunk)
        value = lax.dot_general(
            k_ref[:, pl.ds(c0, chunk)], o_ref[...], (((0,), (0,)), ((), ())),
            preferred_element_type=jnp.float32,
        )
        for piece in range(pieces):
            rows = value[piece * own:(piece + 1) * own]
            for part, order in enumerate(cube.orders):
                at = place(index * pieces + piece, order)
                half = size // 2
                part_sum[pl.ds(at, own), columns[part]] = rows[:, part * half:(part + 1) * half]
        return carry

    lax.fori_loop(0, width // chunk, product, 0)
    plan, _ = halving_plan(width, count)
    starts = halve(cube, part_sum, part_recv, plan, cs, cr)
    mine = jnp.concatenate(
        [
            part_sum[pl.ds(pl.multiple_of(starts[part], own), own), columns[part]]
            for part in range(2)
        ],
        axis=1,
    )
    buf[...] = lax.dot_general(
        mine, mine, (((0,), (0,)), ((), ())), precision=HI, preferred_element_type=jnp.float32
    )
    plan, _ = halving_plan(size, count)
    starts = halve(cube, buf, recv, plan, rs, rr)
    double(cube, buf, full, plan, starts, gs, gr)
    load_augmented(mat, full, size)
    factor(mat, size)
    u_ref[...] = upper_part(mat, size)
    v_ref[...] = mat[:, size:]
    c_ref[pl.ds(pl.multiple_of(cube.seq * own, own), own), :] = lax.dot_general(
        mine, mat[:, size:], (((1,), (1,)), ((), ())), precision=HI,
        preferred_element_type=jnp.float32,
    ).astype(jnp.bfloat16)
    held = [cube.seq]
    sent = []
    index = 0
    for which in reversed(cube.seq_bits):
        copies = []
        for block in held:
            here = c_ref.at[pl.ds(pl.multiple_of(block * own, own), own), :]
            copies.append(cube.copy(here, here, as_.at[index], ar.at[index], which))
            index += 1
        for copy in copies:
            copy.start()
        for copy in copies:
            copy.wait_recv()
        sent += copies
        step = (1 - 2 * cube.bit(which)) * (1 << which[1])
        held = held + [block + step for block in held]
    for copy in sent:
        copy.wait_send()


def coefficient_stage(keys, ortho, seq_count, head_count):
    width = keys.shape[1]
    size = ortho.shape[1]
    count = log2(seq_count * head_count)
    _, total = halving_plan(width, count)
    sems = pltpu.SemaphoreType.DMA((count, 2))
    more = pltpu.SemaphoreType.DMA((seq_count - 1,))
    square = jax.ShapeDtypeStruct((size, size), jnp.float32)
    vmem = pl.BlockSpec(memory_space=pltpu.VMEM)
    return pl.pallas_call(
        functools.partial(second_kernel, seq_count, head_count),
        out_shape=[
            jax.ShapeDtypeStruct((width // head_count, size), jnp.bfloat16), square, square,
        ],
        in_specs=[vmem] * 2,
        out_specs=[vmem] * 3,
        scratch_shapes=[
            pltpu.VMEM((width, size), jnp.float32),
            pltpu.VMEM((total, size), jnp.float32),
        ]
        + scratch_of(size, count)
        + [sems, sems, more, more],
        compiler_params=pltpu.CompilerParams(
            collective_id=1, has_side_effects=True, vmem_limit_bytes=50 << 20
        ),
        cost_estimate=pl.CostEstimate(
            flops=100_000_000_000, bytes_accessed=20_000_000, transcendentals=0
        ),
    )(keys, ortho)


def per_device(cached_keys, sketch_matrix, cached_values, queries, new_keys, new_values):
    highest = lax.Precision.HIGHEST
    seq_count = lax.axis_size("seq")
    head_count = lax.axis_size("head")
    tok_rows = cached_keys.shape[0]
    sketch_rank = sketch_matrix.shape[1]
    rows_with_rows = (((1,), (1,)), ((), ()))
    sketch = jnp.dot(cached_keys, sketch_matrix, preferred_element_type=jnp.float32)
    sketch_group = lax.all_gather(sketch, "head", axis=0, tiled=True)
    gram_first = jnp.dot(sketch.T, sketch, precision=highest)
    inverse_first = summed_inverse(gram_first, seq_count, head_count)
    orthonormal = lax.dot_general(sketch, inverse_first, rows_with_rows, precision=highest)
    stored_ortho = orthonormal.astype(jnp.bfloat16)
    coefficients, upper_second, inverse_second = coefficient_stage(
        cached_keys, stored_ortho, seq_count, head_count
    )
    both = lax.dot_general(upper_second, inverse_first, (((1,), (0,)), ((), ())), precision=highest)
    group_bases = lax.dot_general(
        sketch_group, both, rows_with_rows, precision=highest
    ).astype(jnp.bfloat16)
    key_bases = lax.dynamic_slice_in_dim(
        group_bases, lax.axis_index("head") * tok_rows, tok_rows, 0
    )
    heads_here, query_rows, head_dim = queries.shape
    rows_layer = STEPS * GQA
    score_scale = 1.0 / math.sqrt(head_dim)
    query_view = queries.reshape(heads_here, LAYERS, rows_layer, head_dim)
    coef_view = coefficients.reshape(heads_here, LAYERS, head_dim, sketch_rank)
    absorbed = (
        jnp.einsum("klqh,klhr->klqr", query_view, coef_view, preferred_element_type=jnp.float32)
        * score_scale
    ).astype(jnp.bfloat16)
    flat_queries = absorbed.reshape(heads_here * query_rows, sketch_rank)
    cache_scores = lax.dot_general(
        flat_queries,
        group_bases,
        (((1,), (1,)), ((), ())),
        preferred_element_type=jnp.float32,
    )
    local_peak = jnp.max(cache_scores, axis=1)
    cache_weights = jnp.exp(cache_scores - local_peak[:, None])
    local_total = jnp.sum(cache_weights, axis=1)
    weights_bf = cache_weights.astype(jnp.bfloat16).reshape(heads_here, LAYERS, rows_layer, -1)
    value_view = cached_values.reshape(cached_values.shape[0], heads_here, LAYERS, head_dim)
    numerator = jnp.einsum(
        "klqn,nklh->klqh", weights_bf, value_view, preferred_element_type=jnp.float32
    ).reshape(heads_here, query_rows, head_dim)
    own_rows = query_rows // seq_count
    row_begin = lax.axis_index("seq") * own_rows
    packed = jnp.concatenate(
        [
            numerator,
            jnp.broadcast_to(local_peak.reshape(heads_here, query_rows, 1), (heads_here, query_rows, 64)),
            jnp.broadcast_to(local_total.reshape(heads_here, query_rows, 1), (heads_here, query_rows, 64)),
        ],
        axis=2,
    )
    packed = packed.reshape(heads_here, seq_count, own_rows, 2 * head_dim).transpose(1, 0, 2, 3)
    packed = lax.all_to_all(packed, "seq", 0, 0)
    part_peaks = packed[..., head_dim]
    row_peaks = jnp.max(part_peaks, axis=0)
    part_factor = jnp.exp(part_peaks - row_peaks)
    totals = jnp.sum(part_factor * packed[..., head_dim + 64], axis=0)
    numerator = jnp.sum(part_factor[..., None] * packed[..., :head_dim], axis=0)
    row_index = row_begin + jnp.arange(own_rows, dtype=jnp.int32)
    layer_of_row = row_index // rows_layer
    step_of_row = row_index // GQA % STEPS
    layer_pick = (layer_of_row[:, None] == jnp.arange(LAYERS, dtype=jnp.int32)[None, :]).astype(
        jnp.float32
    )
    allowed = step_of_row[:, None] >= jnp.arange(STEPS, dtype=jnp.int32)[None, :]
    own_queries = lax.dynamic_slice_in_dim(queries, row_begin, own_rows, 1)
    fresh_keys = new_keys.reshape(STEPS, heads_here, LAYERS, head_dim)
    fresh_all = (
        jnp.einsum("kqh,uklh->kqul", own_queries, fresh_keys, preferred_element_type=jnp.float32)
        * score_scale
    )
    fresh_scores = jnp.sum(fresh_all * layer_pick[None, :, None, :], axis=3)
    fresh_scores = jnp.where(allowed[None], fresh_scores, -jnp.inf)
    overall = jnp.maximum(row_peaks, jnp.max(fresh_scores, axis=2))
    cache_factor = jnp.exp(row_peaks - overall)
    fresh_weights = jnp.exp(fresh_scores - overall[..., None])
    fresh_vals = jnp.transpose(
        new_values.astype(jnp.float32).reshape(STEPS, heads_here, LAYERS, head_dim), (1, 0, 2, 3)
    )
    picked = jnp.sum(layer_pick[None, :, None, :, None] * fresh_vals[:, None], axis=3)
    fresh_part = jnp.sum(fresh_weights[..., None] * picked, axis=2)
    softmax_total = totals * cache_factor + jnp.sum(fresh_weights, axis=2)
    attended = (
        (numerator * cache_factor[..., None] + fresh_part) / softmax_total[..., None]
    ).astype(jnp.bfloat16)
    return (attended, key_bases, coefficients)


def solution(mesh):
    placed = (
        P(("seq", "head"), None),
        P(),
        P("seq", "head"),
        P("head", None, None),
        P(None, "head"),
        P(None, "head"),
    )
    return jax.shard_map(
        per_device,
        mesh=mesh,
        in_specs=placed,
        out_specs=(P("head", "seq", None), P(("seq", "head"), None), P("head", None)),
        check_vma=False,
    )
```

```python
import functools
import math

import jax
import jax.numpy as jnp
from jax import lax
from jax.experimental import pallas as pl
from jax.experimental.pallas import tpu as pltpu
from jax.sharding import PartitionSpec as P

GQA = 8
LAYERS = 4
STEPS = 4
HI = lax.Precision.HIGHEST
BLK = 128

def eliminate(square):
    groups = BLK // 8
    sub = lax.broadcasted_iota(jnp.int32, (8, BLK), 0)
    lane = lax.broadcasted_iota(jnp.int32, (8, BLK), 1)
    s = [square[8 * g:8 * g + 8, :] for g in range(groups)]
    w = [(lane == sub + 8 * g).astype(jnp.float32) for g in range(groups)]

    def spread_row(value, p):
        return jnp.broadcast_to(value[p:p + 1, :], (8, BLK))

    def spread_column(value, j):
        return jnp.broadcast_to(value[:, j:j + 1], (8, BLK))

    out = []
    for g in range(groups):
        diag = [spread_column(s[g], 8 * g + q) for q in range(8)]
        below = [[spread_column(s[h], 8 * g + q) for q in range(8)] for h in range(g + 1, groups)]
        xs, xw = s[g], w[g]
        forward = jnp.zeros((8, BLK), jnp.float32)
        pivots = jnp.ones((8, BLK), jnp.float32)
        for p in range(8):
            pivot = spread_row(diag[p], p)
            factor_of = jnp.where(sub == p, 0.0, diag[p] * (1.0 / pivot))
            forward = jnp.where(sub == p, xw, forward)
            pivots = jnp.where(sub == p, pivot, pivots)
            for q in range(p + 1, 8):
                diag[q] = diag[q] - factor_of * spread_row(diag[q], p)
            xs = xs - factor_of * spread_row(xs, p)
            xw = xw - factor_of * spread_row(xw, p)
        out.append(forward * lax.rsqrt(pivots))
        if g + 1 == groups:
            continue
        scale = 1.0 / pivots
        xs, xw = xs * scale, xw * scale
        rows_s = [spread_row(xs, q) for q in range(8)]
        rows_w = [spread_row(xw, q) for q in range(8)]
        for i, h in enumerate(range(g + 1, groups)):
            change_s = [below[i][q] * rows_s[q] for q in range(8)]
            change_w = [below[i][q] * rows_w[q] for q in range(8)]
            while len(change_s) > 1:
                change_s = [change_s[t] + change_s[t + 1] for t in range(0, len(change_s), 2)]
                change_w = [change_w[t] + change_w[t + 1] for t in range(0, len(change_w), 2)]
            s[h] = s[h] - change_s[0]
            w[h] = w[h] - change_w[0]
    return jnp.concatenate(out, axis=0)


def factor(mat, size):
    n = size // BLK
    lane = lax.broadcasted_iota(jnp.int32, (BLK, 2 * size), 1)

    def panel(k, carry):
        r0 = pl.multiple_of(k * BLK, BLK)
        inv = eliminate(mat[pl.ds(r0, BLK), pl.ds(r0, BLK)])
        solved = jnp.dot(inv, mat[pl.ds(r0, BLK), :], precision=HI, preferred_element_type=jnp.float32)
        mat[pl.ds(r0, BLK), :] = jnp.where(lane >= r0, solved, 0.0)

        def below(i, c):
            i0 = pl.multiple_of(i * BLK, BLK)
            mat[pl.ds(i0, BLK), :] -= lax.dot_general(
                mat[pl.ds(r0, BLK), pl.ds(i0, BLK)], mat[pl.ds(r0, BLK), :],
                (((0,), (0,)), ((), ())), precision=HI, preferred_element_type=jnp.float32)
            return c
        lax.fori_loop(k + 1, n, below, 0)
        return carry
    lax.fori_loop(0, n, panel, 0)

def log2(count):
    return count.bit_length() - 1


class Hypercube:
    def __init__(self, seq_count, head_count):
        self.seq = lax.axis_index("seq")
        self.head = lax.axis_index("head")
        self.seq_bits = [("seq", k) for k in range(log2(seq_count))]
        self.head_bits = [("head", k) for k in range(log2(head_count))]
        rest = self.seq_bits[1:] + self.head_bits
        swapped = self.seq_bits[1:][::-1] + self.head_bits[::-1]
        self.orders = [self.seq_bits[:1] + rest, self.seq_bits[:1] + swapped]

    def bit(self, which):
        axis, k = which
        return (self.seq if axis == "seq" else self.head) // (1 << k) % 2

    def partner(self, which):
        axis, k = which
        step = (1 - 2 * self.bit(which)) * (1 << k)
        if axis == "seq":
            return (self.seq + step, self.head)
        return (self.seq, self.head + step)

    def greet(self):
        barrier = pltpu.get_barrier_semaphore()
        bits = self.seq_bits + self.head_bits
        for which in bits:
            pl.semaphore_signal(
                barrier, inc=1, device_id=self.partner(which), device_id_type=pl.DeviceIdType.MESH
            )
        pl.semaphore_wait(barrier, len(bits))

    def copy(self, source, target, send_sem, recv_sem, which):
        return pltpu.make_async_remote_copy(
            src_ref=source,
            dst_ref=target,
            send_sem=send_sem,
            recv_sem=recv_sem,
            device_id=self.partner(which),
            device_id_type=pl.DeviceIdType.MESH,
        )


def add_rows(target, start, source, offset, rows, columns):
    step = min(rows, 64)

    def add(i, carry):
        t0 = pl.multiple_of(start + i * step, step)
        s0 = pl.multiple_of(offset + i * step, step)
        target[pl.ds(t0, step), columns] += source[pl.ds(s0, step), columns]
        return carry

    lax.fori_loop(0, rows // step, add, 0)


def part_columns(width):
    return [pl.ds(0, width // 2), pl.ds(width // 2, width // 2)]


def halving_plan(rows, count):
    plan, offset = [], 0
    for _ in range(count):
        split = rows >= 16
        rows = rows // 2 if split else rows
        plan.append((split, rows, offset))
        offset += rows
    return plan, offset


def halve(cube, buf, recv, plan, send_sem, recv_sem, meanwhile=None):
    columns = part_columns(buf.shape[1])
    starts = [0, 0]
    sent = []
    for level, (split, rows, offset) in enumerate(plan):
        copies = []
        for part, order in enumerate(cube.orders):
            which = order[level]
            bit = cube.bit(which)
            go = starts[part] + (1 - bit) * rows if split else starts[part]
            if split:
                starts[part] = starts[part] + bit * rows
            copies.append(
                cube.copy(
                    buf.at[pl.ds(pl.multiple_of(go, 8), rows), columns[part]],
                    recv.at[pl.ds(offset, rows), columns[part]],
                    send_sem.at[level, part],
                    recv_sem.at[level, part],
                    which,
                )
            )
        for copy in copies:
            copy.start()
        if level == 0 and meanwhile is not None:
            meanwhile()
        for part, copy in enumerate(copies):
            copy.wait_recv()
            if not split:
                copy.wait_send()
            else:
                sent.append(copy)
            add_rows(buf, starts[part], recv, offset, rows, columns[part])
    for copy in sent:
        copy.wait_send()
    return starts


def double(cube, buf, full, plan, starts, send_sem, recv_sem):
    columns = part_columns(buf.shape[1])
    rows = plan[-1][1]
    for part in range(2):
        here = pl.ds(pl.multiple_of(starts[part], 8), rows)
        full[here, columns[part]] = buf[here, columns[part]]
    starts = list(starts)
    sent = []
    for level in reversed(range(len(plan))):
        split, rows, _ = plan[level]
        if not split:
            continue
        copies = []
        for part, order in enumerate(cube.orders):
            which = order[level]
            here = full.at[pl.ds(pl.multiple_of(starts[part], 8), rows), columns[part]]
            copies.append(
                cube.copy(here, here, send_sem.at[level, part], recv_sem.at[level, part], which)
            )
            starts[part] = starts[part] - cube.bit(which) * rows
        for copy in copies:
            copy.start()
        for copy in copies:
            copy.wait_recv()
        sent += copies
    for copy in sent:
        copy.wait_send()


def load_augmented(mat, full, size):
    r = lax.broadcasted_iota(jnp.int32, (size, size), 0)
    c = lax.broadcasted_iota(jnp.int32, (size, size), 1)
    mat[:, :size] = full[...]
    mat[:, size:] = (r == c).astype(jnp.float32)


def upper_part(mat, size):
    r = lax.broadcasted_iota(jnp.int32, (size, size), 0)
    c = lax.broadcasted_iota(jnp.int32, (size, size), 1)
    return jnp.where(c >= r, mat[:, :size], 0.0)


def first_kernel(seq_count, head_count, g_ref, v_ref, buf, recv, full, mat, rs, rr, gs, gr):
    size = g_ref.shape[0]
    cube = Hypercube(seq_count, head_count)
    cube.greet()
    plan, _ = halving_plan(size, len(cube.orders[0]))
    buf[...] = g_ref[...]
    starts = halve(cube, buf, recv, plan, rs, rr)
    double(cube, buf, full, plan, starts, gs, gr)
    load_augmented(mat, full, size)
    factor(mat, size)
    v_ref[...] = mat[:, size:]


def scratch_of(size, count):
    _, total = halving_plan(size, count)
    sems = pltpu.SemaphoreType.DMA((count, 2))
    return [
        pltpu.VMEM((size, size), jnp.float32),
        pltpu.VMEM((total, size), jnp.float32),
        pltpu.VMEM((size, size), jnp.float32),
        pltpu.VMEM((size, 2 * size), jnp.float32),
        sems,
        sems,
        sems,
        sems,
    ]


def summed_inverse(gram, seq_count, head_count):
    size = gram.shape[0]
    return pl.pallas_call(
        functools.partial(first_kernel, seq_count, head_count),
        out_shape=jax.ShapeDtypeStruct((size, size), jnp.float32),
        in_specs=[pl.BlockSpec(memory_space=pltpu.VMEM)],
        out_specs=pl.BlockSpec(memory_space=pltpu.VMEM),
        scratch_shapes=scratch_of(size, log2(seq_count * head_count)),
        compiler_params=pltpu.CompilerParams(
            collective_id=0, has_side_effects=True, vmem_limit_bytes=24 << 20
        ),
        cost_estimate=pl.CostEstimate(
            flops=100_000_000_000, bytes_accessed=4_000_000, transcendentals=0
        ),
    )(gram)


def second_kernel(
    seq_count, head_count, k_ref, o_ref, c_ref, u_ref, v_ref,
    part_sum, part_recv, buf, recv, full, mat, rs, rr, gs, gr, cs, cr, as_, ar,
):
    size = o_ref.shape[1]
    cube = Hypercube(seq_count, head_count)
    cube.greet()
    columns = part_columns(size)
    width = k_ref.shape[1]
    own = width // (seq_count * head_count)
    count = len(cube.orders[0])
    chunk = max(own, 128)
    pieces = chunk // own

    def place(block, order):
        at = 0
        for level, (axis, k) in enumerate(order):
            bit = block // ((1 << k) * (1 if axis == "seq" else seq_count)) % 2
            at = at + bit * (1 << (count - 1 - level))
        return pl.multiple_of(at * own, own)

    def product(index, carry):
        c0 = pl.multiple_of(index * chunk, chunk)
        value = lax.dot_general(
            k_ref[:, pl.ds(c0, chunk)], o_ref[...], (((0,), (0,)), ((), ())),
            preferred_element_type=jnp.float32,
        )
        for piece in range(pieces):
            rows = value[piece * own:(piece + 1) * own]
            for part, order in enumerate(cube.orders):
                at = place(index * pieces + piece, order)
                half = size // 2
                part_sum[pl.ds(at, own), columns[part]] = rows[:, part * half:(part + 1) * half]
        return carry

    meanwhile = None
    if pieces == 1:
        core = cube.bit(cube.seq_bits[0])

        def products_of(bit):
            def step(index, carry):
                return product(2 * index + bit, carry)

            lax.fori_loop(0, width // chunk // 2, step, 0)

        products_of(1 - core)
        meanwhile = functools.partial(products_of, core)
    else:
        lax.fori_loop(0, width // chunk, product, 0)
    plan, _ = halving_plan(width, count)
    starts = halve(cube, part_sum, part_recv, plan, cs, cr, meanwhile)
    mine = jnp.concatenate(
        [
            part_sum[pl.ds(pl.multiple_of(starts[part], own), own), columns[part]]
            for part in range(2)
        ],
        axis=1,
    )
    buf[...] = lax.dot_general(
        mine, mine, (((0,), (0,)), ((), ())), precision=HI, preferred_element_type=jnp.float32
    )
    plan, _ = halving_plan(size, count)
    starts = halve(cube, buf, recv, plan, rs, rr)
    double(cube, buf, full, plan, starts, gs, gr)
    load_augmented(mat, full, size)
    factor(mat, size)
    u_ref[...] = upper_part(mat, size)
    v_ref[...] = mat[:, size:]
    c_ref[pl.ds(pl.multiple_of(cube.seq * own, own), own), :] = lax.dot_general(
        mine, mat[:, size:], (((1,), (1,)), ((), ())), precision=HI,
        preferred_element_type=jnp.float32,
    ).astype(jnp.bfloat16)
    held = [cube.seq]
    sent = []
    index = 0
    for which in reversed(cube.seq_bits):
        copies = []
        for block in held:
            here = c_ref.at[pl.ds(pl.multiple_of(block * own, own), own), :]
            copies.append(cube.copy(here, here, as_.at[index], ar.at[index], which))
            index += 1
        for copy in copies:
            copy.start()
        for copy in copies:
            copy.wait_recv()
        sent += copies
        step = (1 - 2 * cube.bit(which)) * (1 << which[1])
        held = held + [block + step for block in held]
    for copy in sent:
        copy.wait_send()


def coefficient_stage(keys, ortho, seq_count, head_count):
    width = keys.shape[1]
    size = ortho.shape[1]
    count = log2(seq_count * head_count)
    _, total = halving_plan(width, count)
    sems = pltpu.SemaphoreType.DMA((count, 2))
    more = pltpu.SemaphoreType.DMA((seq_count - 1,))
    square = jax.ShapeDtypeStruct((size, size), jnp.float32)
    vmem = pl.BlockSpec(memory_space=pltpu.VMEM)
    return pl.pallas_call(
        functools.partial(second_kernel, seq_count, head_count),
        out_shape=[
            jax.ShapeDtypeStruct((width // head_count, size), jnp.bfloat16), square, square,
        ],
        in_specs=[vmem] * 2,
        out_specs=[vmem] * 3,
        scratch_shapes=[
            pltpu.VMEM((width, size), jnp.float32),
            pltpu.VMEM((total, size), jnp.float32),
        ]
        + scratch_of(size, count)
        + [sems, sems, more, more],
        compiler_params=pltpu.CompilerParams(
            collective_id=1, has_side_effects=True, vmem_limit_bytes=50 << 20
        ),
        cost_estimate=pl.CostEstimate(
            flops=100_000_000_000, bytes_accessed=20_000_000, transcendentals=0
        ),
    )(keys, ortho)


def per_device(cached_keys, sketch_matrix, cached_values, queries, new_keys, new_values):
    highest = lax.Precision.HIGHEST
    seq_count = lax.axis_size("seq")
    head_count = lax.axis_size("head")
    tok_rows = cached_keys.shape[0]
    sketch_rank = sketch_matrix.shape[1]
    rows_with_rows = (((1,), (1,)), ((), ()))
    sketch = jnp.dot(cached_keys, sketch_matrix, preferred_element_type=jnp.float32)
    sketch_group = lax.all_gather(sketch, "head", axis=0, tiled=True)
    gram_first = jnp.dot(sketch.T, sketch, precision=highest)
    inverse_first = summed_inverse(gram_first, seq_count, head_count)
    orthonormal = lax.dot_general(sketch, inverse_first, rows_with_rows, precision=highest)
    stored_ortho = orthonormal.astype(jnp.bfloat16)
    coefficients, upper_second, inverse_second = coefficient_stage(
        cached_keys, stored_ortho, seq_count, head_count
    )
    both = lax.dot_general(upper_second, inverse_first, (((1,), (0,)), ((), ())), precision=highest)
    group_bases = lax.dot_general(
        sketch_group, both, rows_with_rows, precision=highest
    ).astype(jnp.bfloat16)
    key_bases = lax.dynamic_slice_in_dim(
        group_bases, lax.axis_index("head") * tok_rows, tok_rows, 0
    )
    heads_here, query_rows, head_dim = queries.shape
    rows_layer = STEPS * GQA
    score_scale = 1.0 / math.sqrt(head_dim)
    query_view = queries.reshape(heads_here, LAYERS, rows_layer, head_dim)
    coef_view = coefficients.reshape(heads_here, LAYERS, head_dim, sketch_rank)
    absorbed = (
        jnp.einsum("klqh,klhr->klqr", query_view, coef_view, preferred_element_type=jnp.float32)
        * score_scale
    ).astype(jnp.bfloat16)
    flat_queries = absorbed.reshape(heads_here * query_rows, sketch_rank)
    cache_scores = lax.dot_general(
        flat_queries,
        group_bases,
        (((1,), (1,)), ((), ())),
        preferred_element_type=jnp.float32,
    )
    local_peak = jnp.max(cache_scores, axis=1)
    cache_weights = jnp.exp(cache_scores - local_peak[:, None])
    local_total = jnp.sum(cache_weights, axis=1)
    weights_bf = cache_weights.astype(jnp.bfloat16)
    every = jnp.dot(weights_bf, cached_values, preferred_element_type=jnp.float32)
    numerator = jnp.concatenate(
        [
            every[i * rows_layer:(i + 1) * rows_layer, i * head_dim:(i + 1) * head_dim]
            for i in range(heads_here * LAYERS)
        ],
        axis=0,
    ).reshape(heads_here, query_rows, head_dim)
    own_rows = query_rows // seq_count
    row_begin = lax.axis_index("seq") * own_rows
    packed = jnp.concatenate(
        [
            numerator,
            jnp.broadcast_to(local_peak.reshape(heads_here, query_rows, 1), (heads_here, query_rows, 64)),
            jnp.broadcast_to(local_total.reshape(heads_here, query_rows, 1), (heads_here, query_rows, 64)),
        ],
        axis=2,
    )
    packed = packed.reshape(heads_here, seq_count, own_rows, 2 * head_dim).transpose(1, 0, 2, 3)
    packed = lax.all_to_all(packed, "seq", 0, 0)
    part_peaks = packed[..., head_dim]
    row_peaks = jnp.max(part_peaks, axis=0)
    part_factor = jnp.exp(part_peaks - row_peaks)
    totals = jnp.sum(part_factor * packed[..., head_dim + 64], axis=0)
    numerator = jnp.sum(part_factor[..., None] * packed[..., :head_dim], axis=0)
    row_index = row_begin + jnp.arange(own_rows, dtype=jnp.int32)
    layer_of_row = row_index // rows_layer
    step_of_row = row_index // GQA % STEPS
    layer_pick = (layer_of_row[:, None] == jnp.arange(LAYERS, dtype=jnp.int32)[None, :]).astype(
        jnp.float32
    )
    allowed = step_of_row[:, None] >= jnp.arange(STEPS, dtype=jnp.int32)[None, :]
    own_queries = lax.dynamic_slice_in_dim(queries, row_begin, own_rows, 1)
    fresh_keys = new_keys.reshape(STEPS, heads_here, LAYERS, head_dim)
    fresh_all = (
        jnp.einsum("kqh,uklh->kqul", own_queries, fresh_keys, preferred_element_type=jnp.float32)
        * score_scale
    )
    fresh_scores = jnp.sum(fresh_all * layer_pick[None, :, None, :], axis=3)
    fresh_scores = jnp.where(allowed[None], fresh_scores, -jnp.inf)
    overall = jnp.maximum(row_peaks, jnp.max(fresh_scores, axis=2))
    cache_factor = jnp.exp(row_peaks - overall)
    fresh_weights = jnp.exp(fresh_scores - overall[..., None])
    fresh_vals = jnp.transpose(
        new_values.astype(jnp.float32).reshape(STEPS, heads_here, LAYERS, head_dim), (1, 0, 2, 3)
    )
    picked = jnp.sum(layer_pick[None, :, None, :, None] * fresh_vals[:, None], axis=3)
    fresh_part = jnp.sum(fresh_weights[..., None] * picked, axis=2)
    softmax_total = totals * cache_factor + jnp.sum(fresh_weights, axis=2)
    attended = (
        (numerator * cache_factor[..., None] + fresh_part) / softmax_total[..., None]
    ).astype(jnp.bfloat16)
    return (attended, key_bases, coefficients)


def solution(mesh):
    placed = (
        P(("seq", "head"), None),
        P(),
        P("seq", "head"),
        P("head", None, None),
        P(None, "head"),
        P(None, "head"),
    )
    return jax.shard_map(
        per_device,
        mesh=mesh,
        in_specs=placed,
        out_specs=(P("head", "seq", None), P(("seq", "head"), None), P("head", None)),
        check_vma=False,
    )
```
